32 devices in a mesh: row: 4 (over y, core), col: 8 (over z, x).
Axes of the slice: x: 2, y: 2, z: 4, core: 2. Of those that a mesh axis runs over, the one named last changes fastest.
Arguments:
- inputs: bfloat16 [256, 8192], P(('row', 'col')), may hold values from -6 to 6
- layer_norm_gain: float32 [8192], replicated, may hold values from 0.1 to 1.9
- w_in: bfloat16 [8192, 16384], P('row', 'col'), may hold values from -0.09375 to 0.09375
- w_out: bfloat16 [16384, 8192], P('col', 'row'), may hold values from -0.0625 to 0.0625
- pattern_in: int32 [64, 16], replicated, may hold values from 0 to 31, as said below
- pattern_out: int32 [32, 32], replicated, may hold values from 0 to 63, as said below
- out_grad: bfloat16 [256, 8192], P(('row', 'col')), may hold values from -6 to 6
Outputs:
- output: bfloat16 [256, 8192], P(('row', 'col'))
- grad_inputs: bfloat16 [256, 8192], P(('row', 'col'))
- grad_w_in: bfloat16 [8192, 16384], P('row', 'col')
- grad_w_out: bfloat16 [16384, 8192], P('col', 'row')
- norm_gain_gradient: float32 [8192], replicated
The draws below stay inside these ranges and needn't reach their ends.
Inputs may be any that keep to these rules, and one draw needn't show every extreme that they name: `pattern_in`: each row lists 8192 / 512 different tile rows in increasing order. `pattern_out`: each row lists 16384 / 512 different tile rows in increasing order.
All inputs are finite; a program needn't handle non-finite values.
Results may differ from the reference program's by a relative error of at most 0.022.
Values may be sent and summed in bfloat16 or wider, within the bound.
No kernel may reach another device: no remote copies, remote signals or barrier semaphores. Data moves between devices by JAX's collectives and lax.ppermute only.
A program may use at most 128 MiB of HBM per device.

```python
import jax
import jax.numpy as jnp
from jax import lax

D = 8192
FF = 16384
BLOCK = 256
TOKENS = 256
N_ROW = 4
N_COL = 8


def kept_rows(key, columns, tile_rows):
    keys = jax.random.split(key, columns)
    orders = jax.vmap(lambda k: jax.random.permutation(k, tile_rows))(keys)
    return jnp.sort(orders[:, :tile_rows // 2], axis=1).astype(jnp.int32)


def draw_pattern_in(key, part):
    return kept_rows(jax.random.fold_in(key, 11), FF // BLOCK, D // BLOCK)


def draw_pattern_out(key, part):
    return kept_rows(jax.random.fold_in(key, 23), D // BLOCK, FF // BLOCK)


def block_scale(own_key, shape, shards, low, high):
    loudness = 1.0
    for position, shards_of in shards:
        heights = jax.random.uniform(jax.random.fold_in(jax.random.fold_in(own_key, 6), position), (shards_of,), jnp.float32, low / len(shards), high / len(shards))
        loudness = loudness * jnp.repeat(jnp.exp(heights), shape[position] // shards_of).reshape((-1,) + (1,) * (len(shape) - 1 - position))
    return loudness


def gaussian(rng, extent, scale, most, cuts=(), held_as=jnp.bfloat16):
    loudness = block_scale(rng, extent, cuts, -0.22, 0.18) if cuts else 1.0
    array = jax.random.normal(rng, extent, jnp.float32) * scale * loudness
    return jnp.minimum(jnp.maximum(array, -most), most).astype(held_as)


def setup_inputs(seed: int = 0) -> dict:
    key_list = jax.random.split(jax.random.key(seed), 8)
    inputs = gaussian(key_list[0], (TOKENS, D), 1.0, 6.0, ((0, 32),))
    layer_norm_gain = jnp.clip(1.0 + 0.18 * jax.random.normal(key_list[1], (D,), jnp.float32), 0.1, 1.9)
    w_in = gaussian(key_list[2], (D, FF), (D // 2) ** -0.5, 0.09375, ((0, 4), (1, 8)))
    w_out = gaussian(key_list[3], (FF, D), (FF // 2) ** -0.5, 0.0625, ((0, 8), (1, 4)))
    pattern_in = draw_pattern_in(jax.random.fold_in(key_list[7], 71), 0)
    pattern_out = draw_pattern_out(jax.random.fold_in(key_list[7], 71), 0)
    out_grad = gaussian(key_list[6], (TOKENS, D), 1.0, 6.0, ((0, 32),))
    return dict(inputs=inputs, layer_norm_gain=layer_norm_gain, w_in=w_in, w_out=w_out, pattern_in=pattern_in, pattern_out=pattern_out, out_grad=out_grad)


def block_mask(pattern, tile_rows):
    iota = jnp.arange(tile_rows, dtype=jnp.int32)
    return jnp.any(pattern[None, :, :] == iota[:, None, None], axis=2)

def apply_mask(weight, mask):
    rows_t, cols_t = mask.shape
    shaped = weight.reshape(rows_t, BLOCK, cols_t, BLOCK)
    kept = jnp.where(mask[:, None, :, None], shaped, jnp.zeros((), weight.dtype))
    return kept.reshape(weight.shape)

def gelu_value(h):
    inner = 0.7978845608 * (h + 0.044715 * h * h * h)
    return 0.5 * h * (1.0 + jnp.tanh(inner))

def gelu_slope(h):
    tanh_v = jnp.tanh(0.7978845608 * (h + 0.044715 * h * h * h))
    return 0.5 * (1.0 + tanh_v) + 0.5 * h * (1.0 - tanh_v * tanh_v) * 0.7978845608 * (1.0 + 0.134145 * h * h)

def rounded(value):
    return lax.optimization_barrier(value.astype(jnp.bfloat16)).astype(jnp.float32)

def reference(inputs, layer_norm_gain, w_in, w_out, pattern_in, pattern_out, out_grad):
    xfloat = inputs.astype(jnp.float32)
    centered_input = xfloat - lax.optimization_barrier(jnp.mean(xfloat, axis=1, keepdims=True))
    inverse_deviation = lax.rsqrt(lax.optimization_barrier(jnp.mean(centered_input * centered_input, axis=1, keepdims=True)) + 1e-05)
    standardized_input = centered_input * inverse_deviation
    normalized_input = (standardized_input * layer_norm_gain[None, :]).astype(jnp.bfloat16)
    w_in_e = apply_mask(w_in, block_mask(pattern_in, D // BLOCK))
    mask_out = block_mask(pattern_out, FF // BLOCK)
    w_out_e = apply_mask(w_out, mask_out)
    mask_in = block_mask(pattern_in, D // BLOCK)
    pre = jnp.dot(normalized_input, w_in_e, preferred_element_type=jnp.float32)
    activation = gelu_value(pre).astype(jnp.bfloat16)
    hidden_group = FF // N_COL

    def out_step(running, group):
        part_a = lax.dynamic_slice_in_dim(activation, group * hidden_group, hidden_group, 1)
        part_w = lax.dynamic_slice_in_dim(w_out_e, group * hidden_group, hidden_group, 0)
        return (running + rounded(jnp.dot(part_a, part_w, preferred_element_type=jnp.float32)), None)
    summed, _ = lax.scan(out_step, jnp.zeros((TOKENS, D), jnp.float32), jnp.arange(N_COL, dtype=jnp.int32))
    output = (xfloat + summed).astype(jnp.bfloat16)
    d_act = jnp.dot(out_grad, w_out_e.T, preferred_element_type=jnp.float32)
    d_pre = (d_act * gelu_slope(pre)).astype(jnp.bfloat16)
    panel_size = TOKENS // N_ROW

    def w2_step(running, group):
        part_a = lax.dynamic_slice_in_dim(activation, group * panel_size, panel_size, 0)
        part_g = lax.dynamic_slice_in_dim(out_grad, group * panel_size, panel_size, 0)
        return (running + rounded(jnp.dot(part_a.T, part_g, preferred_element_type=jnp.float32)), None)
    w2_sum, _ = lax.scan(w2_step, jnp.zeros((FF, D), jnp.float32), jnp.arange(N_ROW, dtype=jnp.int32))
    grad_w_out = apply_mask(w2_sum.astype(jnp.bfloat16), mask_out)

    def w1_step(running, group):
        part_x = lax.dynamic_slice_in_dim(normalized_input, group * panel_size, panel_size, 0)
        part_d = lax.dynamic_slice_in_dim(d_pre, group * panel_size, panel_size, 0)
        return (running + rounded(jnp.dot(part_x.T, part_d, preferred_element_type=jnp.float32)), None)
    w1_sum, _ = lax.scan(w1_step, jnp.zeros((D, FF), jnp.float32), jnp.arange(N_ROW, dtype=jnp.int32))
    grad_w_in = apply_mask(w1_sum.astype(jnp.bfloat16), mask_in)

    def dx_step(running, group):
        part_d = lax.dynamic_slice_in_dim(d_pre, group * hidden_group, hidden_group, 1)
        part_w = lax.dynamic_slice_in_dim(w_in_e, group * hidden_group, hidden_group, 1)
        return (running + rounded(jnp.dot(part_d, part_w.T, preferred_element_type=jnp.float32)), None)
    normed_gradient, _ = lax.scan(dx_step, jnp.zeros((TOKENS, D), jnp.float32), jnp.arange(N_COL, dtype=jnp.int32))
    norm_gain_gradient = lax.optimization_barrier(jnp.sum(normed_gradient * standardized_input, axis=0))
    gain_scaled = normed_gradient * layer_norm_gain[None, :]
    backward_result = inverse_deviation * (gain_scaled - lax.optimization_barrier(jnp.mean(gain_scaled, axis=1, keepdims=True)) - standardized_input * lax.optimization_barrier(jnp.mean(gain_scaled * standardized_input, axis=1, keepdims=True)))
    grad_inputs = (out_grad.astype(jnp.float32) + backward_result).astype(jnp.bfloat16)
    return (output, grad_inputs, grad_w_in, grad_w_out, norm_gain_gradient)
```

```python
import jax
import jax.numpy as jnp
from jax import lax
from jax.sharding import PartitionSpec as P

BLOCK = 256
BF16 = jnp.bfloat16
F32 = jnp.float32


def block_mask(pattern, tile_rows):
    iota = jnp.arange(tile_rows, dtype=jnp.int32)
    return jnp.any(pattern[None, :, :] == iota[:, None, None], axis=2)


def apply_mask(weight, mask):
    rows_t, cols_t = mask.shape
    shaped = weight.reshape(rows_t, BLOCK, cols_t, BLOCK)
    kept = jnp.where(mask[:, None, :, None], shaped, jnp.zeros((), weight.dtype))
    return kept.reshape(weight.shape)


def gelu_and_slope(h):
    tanh_v = jnp.tanh(0.7978845608 * (h + 0.044715 * h * h * h))
    value = 0.5 * h * (1.0 + tanh_v)
    slope = 0.5 * (1.0 + tanh_v) + 0.5 * h * (1.0 - tanh_v * tanh_v) * 0.7978845608 * (
        1.0 + 0.134145 * h * h
    )
    return value, slope


def dot(left, right):
    return jnp.dot(left, right, preferred_element_type=F32)


def dot_last(left, right):
    return lax.dot_general(left, right, (((1,), (1,)), ((), ())), preferred_element_type=F32)


def dot_first(left, right):
    return lax.dot_general(left, right, (((0,), (0,)), ((), ())), preferred_element_type=F32)


def swap(value, axis, distance):
    size = lax.axis_size(axis)
    return lax.ppermute(value, axis, [(i, i ^ distance) for i in range(size)])


def halves(value, bit, axis):
    low, high = jnp.split(value, 2, axis=axis)
    return jnp.where(bit, high, low), jnp.where(bit, low, high)


def ordered(mine, other, bit, axis):
    return jnp.where(
        bit,
        jnp.concatenate([other, mine], axis=axis),
        jnp.concatenate([mine, other], axis=axis),
    )


def shards(inputs, layer_norm_gain, w_in, w_out, pattern_in, pattern_out, out_grad):
    n_row = lax.axis_size("row")
    n_col = lax.axis_size("col")
    row_index = lax.axis_index("row")
    col_index = lax.axis_index("col")
    core_bit = row_index % 2 == 1
    far_bit = row_index // 2 == 1
    tok = inputs.shape[0]
    width = inputs.shape[1]
    feat, unit = w_in.shape
    feat_tiles, unit_tiles = feat // BLOCK, unit // BLOCK
    line = [1 << b for b in reversed(range(1, n_col.bit_length() - 1))]

    def to_features(value):
        keep, give = halves(value, far_bit, 1)
        got = swap(give, "row", 2)
        both = ordered(keep, got, far_bit, 0)
        keep, give = halves(both, core_bit, 1)
        return jnp.stack([keep, swap(give, "row", 1)])

    def to_tokens(value):
        got = swap(value[1], "row", 1)
        both = ordered(value[0], got, core_bit, 1)
        keep, give = halves(both, far_bit, 0)
        got = swap(give, "row", 2)
        return ordered(keep, got, far_bit, 1)

    def gather(block):
        own = [block]
        chunks = []
        pairs = [(block, swap(block, "col", 1))]
        for i, distance in enumerate(line):
            got = [swap(v, "col", distance) for v in own] if i == 0 else list(
                swap(jnp.stack(own), "col", distance)
            )
            near = [swap(v, "col", 1) for v in got] if i == 0 else list(
                swap(jnp.stack(got), "col", 1)
            )
            if i == 0:
                chunks.append([block, pairs[0][1], got[0], near[0]])
            else:
                chunks.append([v for pair in zip(got, near) for v in pair])
            own = own + got
        return chunks

    xfloat = inputs.astype(F32)
    centered_input = xfloat - jnp.mean(xfloat, axis=1, keepdims=True)
    inverse_deviation = lax.rsqrt(
        jnp.mean(centered_input * centered_input, axis=1, keepdims=True) + 1e-05
    )
    standardized_input = centered_input * inverse_deviation
    normalized_input = (standardized_input * layer_norm_gain[None, :]).astype(BF16)

    mask_in = lax.dynamic_slice(
        block_mask(pattern_in, width // BLOCK),
        (row_index * feat_tiles, col_index * unit_tiles),
        (feat_tiles, unit_tiles),
    )
    mask_out = lax.dynamic_slice(
        block_mask(pattern_out, n_col * unit_tiles),
        (col_index * unit_tiles, row_index * feat_tiles),
        (unit_tiles, feat_tiles),
    )
    w_in_e = lax.optimization_barrier(apply_mask(w_in, mask_in))
    w_out_e = lax.optimization_barrier(apply_mask(w_out, mask_out))

    x_chunks = gather(to_features(normalized_input))
    g_chunks = gather(to_features(out_grad))

    def sum_over_row(product):
        rounded = product.astype(BF16)
        got = swap(rounded[:, 1], "row", 1)
        pair = product[:, 0] + got.astype(F32)
        far = swap(pair.astype(BF16), "row", 2)
        total = (pair + far.astype(F32)).astype(BF16)
        return jnp.stack([total, swap(total, "row", 1)], axis=1).astype(F32)

    def flat(blocks):
        return jnp.stack(blocks).reshape(-1, blocks[0].shape[-1])

    def shaped(value, count):
        return value.reshape(count, 2, 2 * tok, value.shape[-1])

    acts, d_pres, out_parts, dn_parts = [], [], [], []
    x_flat = [flat(c) for c in x_chunks]
    g_flat = [flat(c) for c in g_chunks]
    for xc, gc, blocks in zip(x_flat, g_flat, x_chunks):
        n = len(blocks)
        pre = sum_over_row(shaped(dot(xc, w_in_e), n)).reshape(-1, unit)
        value, slope = gelu_and_slope(pre)
        act = value.astype(BF16)
        d_act = sum_over_row(shaped(dot_last(gc, w_out_e), n)).reshape(-1, unit)
        d_pre = (d_act * slope).astype(BF16)
        acts.append(act)
        d_pres.append(d_pre)
        out_parts.append(shaped(dot(act, w_out_e), n))
        dn_parts.append(shaped(dot_last(d_pre, w_in_e), n))

    def scatter(parts):
        held = []
        for part in parts:
            pairs = part.reshape((-1, 2) + part.shape[1:])
            got = swap(pairs[:, 1].astype(BF16), "col", 1)
            held.append(pairs[:, 0] + got.astype(F32))
        total = jnp.concatenate(held, axis=0)
        for distance in reversed(line):
            low, high = jnp.split(total, 2, axis=0)
            got = swap(high.astype(BF16), "col", distance)
            total = low + got.astype(F32)
        return total[0]

    summed = scatter(out_parts)
    output = (xfloat + to_tokens(summed.astype(BF16)).astype(F32)).astype(BF16)
    normed_gradient = to_tokens(scatter(dn_parts).astype(BF16)).astype(F32)

    gain_part = sum(
        jnp.sum(part.reshape(-1, feat) * xc.astype(F32), axis=0)
        for part, xc in zip(dn_parts, x_flat)
    )
    for b in range(n_col.bit_length() - 1):
        gain_part = gain_part + swap(gain_part, "col", 1 << b)
    pair = ordered(gain_part, swap(gain_part, "row", 1), core_bit, 0)
    norm_gain_gradient = ordered(pair, swap(pair, "row", 2), far_bit, 0) / layer_norm_gain

    x_all = jnp.concatenate(x_flat)
    g_all = jnp.concatenate(g_flat)
    grad_w_out = apply_mask(dot_first(jnp.concatenate(acts), g_all).astype(BF16), mask_out)
    grad_w_in = apply_mask(dot_first(x_all, jnp.concatenate(d_pres)).astype(BF16), mask_in)

    gain_scaled = normed_gradient * layer_norm_gain[None, :]
    backward_result = inverse_deviation * (
        gain_scaled
        - jnp.mean(gain_scaled, axis=1, keepdims=True)
        - standardized_input * jnp.mean(gain_scaled * standardized_input, axis=1, keepdims=True)
    )
    grad_inputs = (out_grad.astype(F32) + backward_result).astype(BF16)
    return (output, grad_inputs, grad_w_in, grad_w_out, norm_gain_gradient)


def solution(mesh):
    in_specs = (
        P(("row", "col"), None),
        P(),
        P("row", "col"),
        P("col", "row"),
        P(),
        P(),
        P(("row", "col"), None),
    )
    out_specs = (
        P(("row", "col"), None),
        P(("row", "col"), None),
        P("row", "col"),
        P("col", "row"),
        P(),
    )
    return jax.shard_map(shards, mesh=mesh, in_specs=in_specs, out_specs=out_specs, check_vma=False)
```

```python
import functools

import jax
import jax.numpy as jnp
from jax import lax
from jax.experimental import pallas as pl
from jax.experimental.pallas import tpu as pltpu
from jax.sharding import PartitionSpec as P

BLOCK = 256
PANEL = 1024
BF16 = jnp.bfloat16
F32 = jnp.float32
VMEM = pl.BlockSpec(memory_space=pltpu.VMEM)
SMEM = pl.BlockSpec(memory_space=pltpu.SMEM)
NO_COST = pl.CostEstimate(flops=0, bytes_accessed=0, transcendentals=0)


def kept_tiles(pattern, first_row, rows, first_column, columns):
    own = lax.dynamic_slice_in_dim(pattern, first_column, columns, 0)
    iota = first_row + jnp.arange(rows, dtype=jnp.int32)
    return jnp.any(own[None, :, :] == iota[:, None, None], axis=2).astype(jnp.int32)


def masked(keep_tile, value):
    return jnp.where(keep_tile == 1, value, jnp.zeros_like(value))


def keep_kernel(mask_ref, weight_ref, out_ref, copied):
    rows, columns = mask_ref.shape

    def each(kept, other):
        @pl.loop(0, rows)
        def _(i):
            for j in range(columns):
                here = (pl.ds(pl.multiple_of(i * BLOCK, BLOCK), BLOCK), pl.ds(j * BLOCK, BLOCK))

                @pl.when(mask_ref[i, j] == 1)
                def _():
                    kept(pltpu.make_async_copy(weight_ref.at[here], out_ref.at[here], copied.at[i, j]))

                if other is not None:

                    @pl.when(mask_ref[i, j] != 1)
                    def _():
                        other(here)

    def clear(here):
        out_ref[here] = jnp.zeros((BLOCK, BLOCK), out_ref.dtype)

    each(lambda copy: copy.start(), clear)
    each(lambda copy: copy.wait(), None)


def keep(weight, mask):
    return pl.pallas_call(
        keep_kernel,
        out_shape=pltpu.VMEM(weight.shape, weight.dtype),
        in_specs=[SMEM, pl.BlockSpec(memory_space=pltpu.HBM)],
        out_specs=VMEM,
        scratch_shapes=[pltpu.SemaphoreType.DMA(mask.shape)],
        compiler_params=pltpu.CompilerParams(vmem_limit_bytes=2 << 20),
        cost_estimate=NO_COST,
    )(mask, pltpu.with_memory_space_constraint(weight, pltpu.HBM))


def product_kernel(left_ref, weight_ref, out_ref):
    width = weight_ref.shape[1]
    panel = min(PANEL, width)

    @pl.loop(0, width // panel)
    def _(k):
        here = pl.ds(pl.multiple_of(k * panel, panel), panel)
        out_ref[:, here] = jnp.dot(
            left_ref[...], weight_ref[:, here], preferred_element_type=F32
        )


def product(left, weight):
    return pl.pallas_call(
        product_kernel,
        out_shape=jax.ShapeDtypeStruct((left.shape[0], weight.shape[1]), F32),
        in_specs=[VMEM, VMEM],
        out_specs=VMEM,
        compiler_params=pltpu.CompilerParams(vmem_limit_bytes=6 << 20),
        cost_estimate=NO_COST,
    )(left, pltpu.with_memory_space_constraint(weight, pltpu.VMEM))


def outer_kernel(mask_ref, left_ref, right_ref, out_ref):
    i = pl.program_id(0)
    tiles = out_ref.shape[0] // BLOCK
    turned = left_ref[...].T
    for j in range(out_ref.shape[1] // BLOCK):
        here = slice(j * BLOCK, (j + 1) * BLOCK)
        full = jnp.dot(turned, right_ref[:, here], preferred_element_type=F32)
        for t in range(tiles):
            rows = slice(t * BLOCK, (t + 1) * BLOCK)
            out_ref[rows, here] = masked(mask_ref[i * tiles + t, j], full[rows]).astype(
                out_ref.dtype
            )


def outer(left, right, mask):
    tokens, rows = left.shape
    columns = right.shape[1]
    step = 2 * BLOCK
    return pl.pallas_call(
        outer_kernel,
        grid=(rows // step,),
        out_shape=jax.ShapeDtypeStruct((rows, columns), BF16),
        in_specs=[
            SMEM,
            pl.BlockSpec((tokens, step), lambda i: (0, i)),
            pl.BlockSpec((tokens, columns), lambda i: (0, 0)),
        ],
        out_specs=pl.BlockSpec((step, columns), lambda i: (i, 0)),
        compiler_params=pltpu.CompilerParams(vmem_limit_bytes=12 << 20),
        cost_estimate=NO_COST,
    )(mask, left, right)


def normalise_kernel(
    far_ref, input_hbm, gain_hbm, kept_ref, given_ref, standard_ref, deviation_ref, input_ref, gain_ref, copied
):
    copies = [
        pltpu.make_async_copy(input_hbm, input_ref, copied.at[0]),
        pltpu.make_async_copy(gain_hbm, gain_ref, copied.at[1]),
    ]
    for copy in copies:
        copy.start()
    for copy in copies:
        copy.wait()
    xfloat = input_ref[...].astype(F32)
    centered = xfloat - jnp.mean(xfloat, axis=1, keepdims=True)
    deviation = lax.rsqrt(jnp.mean(centered * centered, axis=1, keepdims=True) + 1e-05)
    standard = centered * deviation
    normed = standard * gain_ref[...]
    half = normed.shape[1] // 2
    low, high = normed[:, :half], normed[:, half:]
    far = far_ref[0] == 1
    kept_ref[...] = jnp.where(far, high, low).astype(BF16)
    given_ref[...] = jnp.where(far, low, high).astype(BF16)
    standard_ref[...] = standard
    deviation_ref[...] = deviation


def normalise(inputs, gain, far):
    tok, width = inputs.shape
    half = jax.ShapeDtypeStruct((tok, width // 2), BF16)
    return pl.pallas_call(
        normalise_kernel,
        out_shape=(
            half,
            half,
            jax.ShapeDtypeStruct((tok, width), F32),
            jax.ShapeDtypeStruct((tok, 1), F32),
        ),
        in_specs=[SMEM] + [pl.BlockSpec(memory_space=pltpu.HBM)] * 2,
        out_specs=(VMEM,) * 4,
        scratch_shapes=[
            pltpu.VMEM(inputs.shape, inputs.dtype),
            pltpu.VMEM(gain.shape, gain.dtype),
            pltpu.SemaphoreType.DMA((2,)),
        ],
        compiler_params=pltpu.CompilerParams(vmem_limit_bytes=6 << 20),
        cost_estimate=NO_COST,
    )(far, *(pltpu.with_memory_space_constraint(v, pltpu.HBM) for v in (inputs, gain)))


def turn_kernel(weight_ref, out_ref):
    columns = weight_ref.shape[1]

    @pl.loop(0, columns // BLOCK)
    def _(k):
        here = pl.ds(pl.multiple_of(k * BLOCK, BLOCK), BLOCK)
        out_ref[here, :] = weight_ref[:, here].T


def turn(weight):
    return pl.pallas_call(
        turn_kernel,
        out_shape=pltpu.VMEM(weight.shape[::-1], weight.dtype),
        in_specs=[VMEM],
        out_specs=VMEM,
        compiler_params=pltpu.CompilerParams(vmem_limit_bytes=6 << 20),
        cost_estimate=NO_COST,
    )(pltpu.with_memory_space_constraint(weight, pltpu.VMEM))


def gelu_and_slope(h):
    tanh_v = jnp.tanh(0.7978845608 * (h + 0.044715 * h * h * h))
    value = 0.5 * h * (1.0 + tanh_v)
    slope = 0.5 * (1.0 + tanh_v) + 0.5 * h * (1.0 - tanh_v * tanh_v) * 0.7978845608 * (
        1.0 + 0.134145 * h * h
    )
    return value, slope


def swap(value, axis, distance):
    size = lax.axis_size(axis)
    return lax.ppermute(value, axis, [(i, i ^ distance) for i in range(size)])


def halves(value, bit, axis):
    low, high = jnp.split(value, 2, axis=axis)
    return jnp.where(bit, high, low), jnp.where(bit, low, high)


def ordered(mine, other, bit, axis):
    return jnp.where(
        bit,
        jnp.concatenate([other, mine], axis=axis),
        jnp.concatenate([mine, other], axis=axis),
    )


class Plan:
    def __init__(self, staged):
        self.staged = staged
        self.tasks = []

    def work(self, stage, function, *deps):
        self.tasks.append((stage if self.staged else 0, function, deps))
        return len(self.tasks) - 1

    def swap(self, stage, axis, distance, dep):
        return self.work(stage, functools.partial(swap, axis=axis, distance=distance), dep)

    def run(self, results):
        values = {}
        for stage in sorted({t[0] for t in self.tasks}):
            for task, (when, function, deps) in enumerate(self.tasks):
                if when == stage:
                    values[task] = function(*(values[d] for d in deps))
            wanted = {d for when, _, deps in self.tasks if when > stage for d in deps}
            live = sorted((wanted | set(results)) & set(values))
            values.update(zip(live, lax.optimization_barrier(tuple(values[n] for n in live))))
        return tuple(values[n] for n in results)


def second(pair):
    return pair[1]


def to_bf16(value):
    return value.astype(BF16)


def shards(inputs, layer_norm_gain, w_in, w_out, pattern_in, pattern_out, out_grad):
    n_col = lax.axis_size("col")
    row_index = lax.axis_index("row")
    col_index = lax.axis_index("col")
    core_bit = row_index % 2 == 1
    far_bit = row_index // 2 == 1
    tok = inputs.shape[0]
    feat, unit = w_in.shape
    feat_tiles, unit_tiles = feat // BLOCK, unit // BLOCK
    line = [1 << b for b in reversed(range(1, n_col.bit_length() - 1))]
    last = len(line)
    places = [2] + [1 << i for i in range(1, last)]

    plan = Plan(last == 2)
    work, swapped = plan.work, plan.swap

    def to_core(v, got):
        return halves(ordered(v[0], got, far_bit, 0), core_bit, 1)

    g0 = work(0, lambda: halves(out_grad, far_bit, 1))
    gfar = swapped(0, "row", 2, work(0, second, g0))
    x0 = work(
        0,
        lambda: normalise(inputs, layer_norm_gain[None, :], far_bit.astype(jnp.int32)[None]),
    )
    xfar = swapped(0, "row", 2, work(0, second, x0))
    x1, g1 = work(0, to_core, x0, xfar), work(0, to_core, g0, gfar)
    core = swapped(0, "row", 1, work(0, lambda x, g: jnp.stack([x[1], g[1]]), x1, g1))
    xown = work(0, lambda v, got: jnp.stack([v[0], got[0]])[None], x1, core)
    gown = work(0, lambda v, got: jnp.stack([v[0], got[1]])[None], g1, core)

    mask_in = work(1, lambda: kept_tiles(
        pattern_in, row_index * feat_tiles, feat_tiles, col_index * unit_tiles, unit_tiles
    ))
    mask_out = work(1, lambda: kept_tiles(
        pattern_out, col_index * unit_tiles, unit_tiles, row_index * feat_tiles, feat_tiles
    ))
    in_e = work(1, lambda mask: keep(w_in, mask), mask_in)
    out_e = work(2, lambda mask: keep(w_out, mask), mask_out)

    def give_half(*parts):
        return jnp.concatenate([v[v.shape[0] // 2 :] for v in parts]).astype(BF16)

    def add_half(*parts):
        kept = jnp.concatenate([v[: v.shape[0] // 2] for v in parts[:-1]])
        return kept + parts[-1].astype(F32)

    def row_sum(stages, parts, sizes):
        first, core_stage, back, unpack = stages
        got = swapped(core_stage, "row", 1, work(first, give_half, *parts))
        pair = work(core_stage, add_half, *parts, got)
        rounded = work(core_stage, to_bf16, pair)
        far = swapped(core_stage, "row", 2, rounded)
        total = work(back, lambda v, got: (v + got.astype(F32)).astype(BF16), pair, far)
        other = swapped(back, "row", 1, total)
        sums, start = [], 0
        for size in sizes:
            rows = slice(start, start + size)
            start = rows.stop
            sums.append(work(
                unpack,
                lambda v, got, rows=rows: jnp.concatenate([v[rows], got[rows]]).astype(F32),
                total,
                other,
            ))
        return sums, rounded

    def chunk(*parts):
        return jnp.concatenate(parts).swapaxes(0, 1).reshape(-1, feat)

    def join(*parts):
        return jnp.concatenate(parts)

    def behind(value, *others):
        return lax.optimization_barrier((value,) + others)[0]

    near = swapped(1, "col", 1, work(1, join, xown, gown))
    xline, gline = [swapped(1, "col", line[0], xown)], []
    xnear, gnear = [swapped(2, "col", 1, xline[0])], []
    xheld, gheld = [xown, xline[0]], [gown]
    xfirst, gfirst = work(2, lambda v: v[:1], near), work(2, lambda v: v[1:], near)
    for i in range(1, last):
        xline.append(swapped(1 + i, "col", line[i], work(1 + i, join, *xheld)))
        xheld.append(xline[i])
    gline.append(swapped(2, "col", line[0], gown))
    gheld.append(gline[0])
    sizes = [n * 4 * tok for n in places]
    xc = [work(2, chunk, xown, xfirst, xline[0], xnear[0])]
    xp = [work(2, product, xc[0], in_e)]
    (total,), rounded = row_sum((2, 3, 4, 4), xp, sizes[:1])
    pre = [total]
    for i in range(1, last):
        gnear.append(swapped(2 + i, "col", 1, gline[i - 1]))
        xnear.append(swapped(2 + i, "col", 1, xline[i]))
        held = work(2 + i, join, *gheld)
        gline.append(swapped(2 + i, "col", line[i], work(2 + i, behind, held, rounded)))
        gheld.append(gline[i])
    out_t = work(3, turn, out_e)
    gc = [work(3, chunk, gown, gfirst, gline[0], gnear[0])]
    gp = [work(3, product, gc[0], out_t)]
    gnear.append(swapped(4, "col", 1, gline[-1]))
    d_act = []
    for i in range(1, last):
        xc.append(work(4, chunk, xline[i], xnear[i]))
        xp.append(work(4, product, xc[i], in_e))
        sums, rounded = row_sum(
            (4, 4, 5, 5), [xp[i], gp[i - 1]], [sizes[i], sizes[i - 1]]
        )
        pre.append(sums[0])
        d_act.append(sums[1])
        late = work(4, behind, gline[i], rounded)
        gc.append(work(4, chunk, late, gnear[i]))
        gp.append(work(4, product, gc[i], out_t))
    in_t = work(4, turn, in_e)
    d_act.append(row_sum((4, 5, 6, 6), gp[-1:], sizes[-1:])[0][0])

    def forward(pre):
        value, slope = gelu_and_slope(pre)
        return value.astype(BF16), slope

    def places_first(value):
        return value.reshape(2, -1, 2 * tok, value.shape[-1]).swapaxes(0, 1)

    def give_near(i, v):
        v = places_first(v)
        return (v[v.shape[0] // 2 :] if i else v[1::2]).astype(BF16)

    def keep_near(i, v, got):
        v = places_first(v)
        return (v[: v.shape[0] // 2] if i else v[::2]) + got.astype(F32)

    made = [work(4 + i, forward, pre[i]) for i in range(last)]
    act = [work(4 + i, lambda v: v[0], made[i]) for i in range(last)]
    yp = [work(4 + i, product, act[i], out_e) for i in range(last)]
    ygive = [work(4 + i, functools.partial(give_near, i), yp[i]) for i in range(last)]
    ynear = [swapped(4 + i, "col", 1, ygive[i]) for i in range(last)]
    d_pre = [
        work(5 + i, lambda v, made: (v * made[1]).astype(BF16), d_act[i], made[i])
        for i in range(last)
    ]
    np_ = [work(5 + i, product, d_pre[i], in_t) for i in range(last)]
    last_give = work(4 + last, functools.partial(give_near, last - 1), np_[-1])

    def add(v, got):
        return v + got

    def gain_terms(*parts):
        left, right = parts[:last], parts[last:]
        return sum(jnp.sum(n * x.astype(F32), axis=0) for n, x in zip(left, right))

    gain = work(6, gain_terms, *np_, *xc)
    for b, distance in enumerate([1] + line[::-1]):
        gain = work(min(7 + b, 9), add, gain, swapped(min(6 + b, 8), "col", distance, gain))

    nnear = [
        swapped(7, "col", 1, work(7, functools.partial(give_near, i), np_[i]))
        for i in range(last - 1)
    ] + [swapped(4 + last, "col", 1, last_give)]

    def line_sum(stage, products, got, late):
        sums = [
            work(
                stage if i or not late else stage + last - 1,
                functools.partial(keep_near, i),
                products[i],
                got[i],
            )
            for i in range(last)
        ]
        for i in reversed(range(1, last)):
            when = stage + last - 1 - i
            moved = swapped(when, "col", line[i], work(when, to_bf16, sums[i]))
            for m in range(i):
                first = sum(places[:m])
                sums[m] = work(
                    when + 1,
                    lambda v, got, first=first: v + got[first : first + v.shape[0]].astype(F32),
                    sums[m],
                    moved,
                )
        give = work(stage + last - 1, lambda v: v[1].astype(BF16), sums[0])
        moved = swapped(stage + last - 1, "col", line[0], give)
        return give, work(
            stage + last, lambda v, got: (v[0] + got.astype(F32)).astype(BF16), sums[0], moved
        )

    def to_far(v, got):
        return halves(ordered(v[0], got, core_bit, 1), far_bit, 0)

    _, y = line_sum(6, yp, ynear, False)
    last_sent, n = line_sum(7, np_, nnear, True)
    y1 = work(8, to_far, y, swapped(8, "row", 1, work(8, second, y)))
    n1 = work(9, to_far, n, swapped(9, "row", 1, work(9, second, n)))
    yfar = swapped(9, "row", 2, work(9, second, y1))
    nfar = swapped(9, "row", 2, work(9, second, n1))
    output = work(9, lambda v, got: (
        inputs.astype(F32) + ordered(v[0], got, far_bit, 1).astype(F32)
    ).astype(BF16), y1, yfar)

    got = swapped(9, "row", 1, gain)
    gain = work(9, lambda v, got: ordered(v, got, core_bit, 0), gain, got)
    gain = work(9, lambda v, other: behind(v, other[0]), gain, n1)
    got = swapped(9, "row", 2, gain)
    gain_gradient = work(
        9, lambda v, got: ordered(v, got, far_bit, 0) / layer_norm_gain, gain, got
    )

    def input_gradient(v, got, made):
        standard, deviation = made[2:]
        scaled = ordered(v[0], got, far_bit, 1).astype(F32) * layer_norm_gain[None, :]
        result = deviation * (
            scaled
            - jnp.mean(scaled, axis=1, keepdims=True)
            - standard * jnp.mean(scaled * standard, axis=1, keepdims=True)
        )
        return (out_grad.astype(F32) + result).astype(BF16)

    grad_inputs = work(9, input_gradient, n1, nfar, x0)

    def weight_gradient(mask, before, *parts):
        left, right = parts[:last], parts[last:]
        return outer(jnp.concatenate(left), jnp.concatenate(right), behind(mask, before))

    grad_w_out = work(4 + last, weight_gradient, mask_out, last_give, *act, *gc)
    grad_w_in = work(8, weight_gradient, mask_in, last_sent, *xc, *d_pre)

    return plan.run((output, grad_inputs, grad_w_in, grad_w_out, gain_gradient))


def solution(mesh):
    in_specs = (
        P(("row", "col"), None),
        P(),
        P("row", "col"),
        P("col", "row"),
        P(),
        P(),
        P(("row", "col"), None),
    )
    out_specs = (
        P(("row", "col"), None),
        P(("row", "col"), None),
        P("row", "col"),
        P("col", "row"),
        P(),
    )
    return jax.shard_map(shards, mesh=mesh, in_specs=in_specs, out_specs=out_specs, check_vma=False)
```

```python
import functools

import jax
import jax.numpy as jnp
from jax import lax
from jax.experimental import pallas as pl
from jax.experimental.pallas import tpu as pltpu
from jax.sharding import PartitionSpec as P

BLOCK = 256
PANEL = 1024
BF16 = jnp.bfloat16
F32 = jnp.float32
VMEM = pl.BlockSpec(memory_space=pltpu.VMEM)
SMEM = pl.BlockSpec(memory_space=pltpu.SMEM)
NO_COST = pl.CostEstimate(flops=0, bytes_accessed=0, transcendentals=0)


def kept_tiles(pattern, first_row, rows, first_column, columns):
    own = lax.dynamic_slice_in_dim(pattern, first_column, columns, 0)
    iota = first_row + jnp.arange(rows, dtype=jnp.int32)
    return jnp.any(own[None, :, :] == iota[:, None, None], axis=2).astype(jnp.int32)


def masked(keep_tile, value):
    return jnp.where(keep_tile == 1, value, jnp.zeros_like(value))


def keep_kernel(mask_ref, weight_ref, out_ref, copied):
    rows, columns = mask_ref.shape

    def each(kept, other):
        @pl.loop(0, rows)
        def _(i):
            for j in range(columns):
                here = (pl.ds(pl.multiple_of(i * BLOCK, BLOCK), BLOCK), pl.ds(j * BLOCK, BLOCK))

                @pl.when(mask_ref[i, j] == 1)
                def _():
                    kept(pltpu.make_async_copy(weight_ref.at[here], out_ref.at[here], copied.at[i, j]))

                if other is not None:

                    @pl.when(mask_ref[i, j] != 1)
                    def _():
                        other(here)

    def clear(here):
        out_ref[here] = jnp.zeros((BLOCK, BLOCK), out_ref.dtype)

    each(lambda copy: copy.start(), clear)
    each(lambda copy: copy.wait(), None)


def keep(weight, mask):
    return pl.pallas_call(
        keep_kernel,
        out_shape=pltpu.VMEM(weight.shape, weight.dtype),
        in_specs=[SMEM, pl.BlockSpec(memory_space=pltpu.HBM)],
        out_specs=VMEM,
        scratch_shapes=[pltpu.SemaphoreType.DMA(mask.shape)],
        compiler_params=pltpu.CompilerParams(vmem_limit_bytes=2 << 20),
        cost_estimate=NO_COST,
    )(mask, pltpu.with_memory_space_constraint(weight, pltpu.HBM))


def product_kernel(left_ref, weight_ref, out_ref):
    width = weight_ref.shape[1]
    panel = min(PANEL, width)

    @pl.loop(0, width // panel)
    def _(k):
        here = pl.ds(pl.multiple_of(k * panel, panel), panel)
        out_ref[:, here] = jnp.dot(
            left_ref[...], weight_ref[:, here], preferred_element_type=F32
        )


def product(left, weight):
    return pl.pallas_call(
        product_kernel,
        out_shape=jax.ShapeDtypeStruct((left.shape[0], weight.shape[1]), F32),
        in_specs=[VMEM, VMEM],
        out_specs=VMEM,
        compiler_params=pltpu.CompilerParams(vmem_limit_bytes=6 << 20),
        cost_estimate=NO_COST,
    )(left, pltpu.with_memory_space_constraint(weight, pltpu.VMEM))


def outer_kernel(mask_ref, left_ref, right_ref, out_ref):
    i = pl.program_id(0)
    tiles = out_ref.shape[0] // BLOCK
    turned = left_ref[...].T
    for j in range(out_ref.shape[1] // BLOCK):
        here = slice(j * BLOCK, (j + 1) * BLOCK)
        full = jnp.dot(turned, right_ref[:, here], preferred_element_type=F32)
        for t in range(tiles):
            rows = slice(t * BLOCK, (t + 1) * BLOCK)
            out_ref[rows, here] = masked(mask_ref[i * tiles + t, j], full[rows]).astype(
                out_ref.dtype
            )


def outer(left, right, mask):
    tokens, rows = left.shape
    columns = right.shape[1]
    step = 2 * BLOCK
    return pl.pallas_call(
        outer_kernel,
        grid=(rows // step,),
        out_shape=jax.ShapeDtypeStruct((rows, columns), BF16),
        in_specs=[
            SMEM,
            pl.BlockSpec((tokens, step), lambda i: (0, i)),
            pl.BlockSpec((tokens, columns), lambda i: (0, 0)),
        ],
        out_specs=pl.BlockSpec((step, columns), lambda i: (i, 0)),
        compiler_params=pltpu.CompilerParams(vmem_limit_bytes=12 << 20),
        cost_estimate=NO_COST,
    )(mask, left, right)


def normalise_kernel(
    far_ref, input_hbm, gain_hbm, kept_ref, given_ref, standard_ref, deviation_ref, input_ref, gain_ref, copied
):
    copies = [
        pltpu.make_async_copy(input_hbm, input_ref, copied.at[0]),
        pltpu.make_async_copy(gain_hbm, gain_ref, copied.at[1]),
    ]
    for copy in copies:
        copy.start()
    for copy in copies:
        copy.wait()
    xfloat = input_ref[...].astype(F32)
    centered = xfloat - jnp.mean(xfloat, axis=1, keepdims=True)
    deviation = lax.rsqrt(jnp.mean(centered * centered, axis=1, keepdims=True) + 1e-05)
    standard = centered * deviation
    normed = standard * gain_ref[...]
    half = normed.shape[1] // 2
    low, high = normed[:, :half], normed[:, half:]
    far = far_ref[0] == 1
    kept_ref[...] = jnp.where(far, high, low).astype(BF16)
    given_ref[...] = jnp.where(far, low, high).astype(BF16)
    standard_ref[...] = standard
    deviation_ref[...] = deviation


def normalise(inputs, gain, far):
    tok, width = inputs.shape
    half = jax.ShapeDtypeStruct((tok, width // 2), BF16)
    return pl.pallas_call(
        normalise_kernel,
        out_shape=(
            half,
            half,
            jax.ShapeDtypeStruct((tok, width), F32),
            jax.ShapeDtypeStruct((tok, 1), F32),
        ),
        in_specs=[SMEM] + [pl.BlockSpec(memory_space=pltpu.HBM)] * 2,
        out_specs=(VMEM,) * 4,
        scratch_shapes=[
            pltpu.VMEM(inputs.shape, inputs.dtype),
            pltpu.VMEM(gain.shape, gain.dtype),
            pltpu.SemaphoreType.DMA((2,)),
        ],
        compiler_params=pltpu.CompilerParams(vmem_limit_bytes=6 << 20),
        cost_estimate=NO_COST,
    )(far, *(pltpu.with_memory_space_constraint(v, pltpu.HBM) for v in (inputs, gain)))


def turn_kernel(weight_ref, out_ref):
    columns = weight_ref.shape[1]

    @pl.loop(0, columns // BLOCK)
    def _(k):
        here = pl.ds(pl.multiple_of(k * BLOCK, BLOCK), BLOCK)
        out_ref[here, :] = weight_ref[:, here].T


def turn(weight):
    return pl.pallas_call(
        turn_kernel,
        out_shape=pltpu.VMEM(weight.shape[::-1], weight.dtype),
        in_specs=[VMEM],
        out_specs=VMEM,
        compiler_params=pltpu.CompilerParams(vmem_limit_bytes=6 << 20),
        cost_estimate=NO_COST,
    )(pltpu.with_memory_space_constraint(weight, pltpu.VMEM))


def gelu_and_slope(h):
    tanh_v = jnp.tanh(0.7978845608 * (h + 0.044715 * h * h * h))
    value = 0.5 * h * (1.0 + tanh_v)
    slope = 0.5 * (1.0 + tanh_v) + 0.5 * h * (1.0 - tanh_v * tanh_v) * 0.7978845608 * (
        1.0 + 0.134145 * h * h
    )
    return value, slope


def swap(value, axis, distance):
    size = lax.axis_size(axis)
    return lax.ppermute(value, axis, [(i, i ^ distance) for i in range(size)])


def halves(value, bit, axis):
    low, high = jnp.split(value, 2, axis=axis)
    return jnp.where(bit, high, low), jnp.where(bit, low, high)


def ordered(mine, other, bit, axis):
    return jnp.where(
        bit,
        jnp.concatenate([other, mine], axis=axis),
        jnp.concatenate([mine, other], axis=axis),
    )


class Plan:
    def __init__(self, staged):
        self.staged = staged
        self.tasks = []

    def work(self, stage, function, *deps):
        self.tasks.append((stage if self.staged else 0, function, deps))
        return len(self.tasks) - 1

    def swap(self, stage, axis, distance, dep):
        return self.work(stage, functools.partial(swap, axis=axis, distance=distance), dep)

    def run(self, results):
        values = {}
        for stage in sorted({t[0] for t in self.tasks}):
            for task, (when, function, deps) in enumerate(self.tasks):
                if when == stage:
                    values[task] = function(*(values[d] for d in deps))
            wanted = {d for when, _, deps in self.tasks if when > stage for d in deps}
            live = sorted((wanted | set(results)) & set(values))
            values.update(zip(live, lax.optimization_barrier(tuple(values[n] for n in live))))
        return tuple(values[n] for n in results)


def first(pair):
    return pair[0]


def second(pair):
    return pair[1]


def to_bf16(value):
    return value.astype(BF16)


def shards(inputs, layer_norm_gain, w_in, w_out, pattern_in, pattern_out, out_grad):
    n_col = lax.axis_size("col")
    row_index = lax.axis_index("row")
    col_index = lax.axis_index("col")
    core_bit = row_index % 2 == 1
    far_bit = row_index // 2 == 1
    tok = inputs.shape[0]
    feat, unit = w_in.shape
    feat_tiles, unit_tiles = feat // BLOCK, unit // BLOCK
    line = [1 << b for b in reversed(range(1, n_col.bit_length() - 1))]
    last = len(line)
    places = [2] + [1 << i for i in range(1, last)]

    plan = Plan(last == 2)
    work, swapped = plan.work, plan.swap

    def to_core(v, got):
        return halves(ordered(v[0], got, far_bit, 0), core_bit, 1)

    def across(stage, dep):
        return swapped(stage, ("row", "col"), 2 * n_col + line[0], dep)

    g0 = work(0, lambda: halves(out_grad, far_bit, 1))
    gfar = swapped(0, "row", 2, work(0, second, g0))
    x0 = work(
        0,
        lambda: normalise(inputs, layer_norm_gain[None, :], far_bit.astype(jnp.int32)[None]),
    )
    xgive = work(0, second, x0)
    xline0 = work(
        0,
        lambda v, got: (v,  got),
        swapped(0, "col", line[0], work(0, first, x0)),
        across(0, xgive),
    )
    xfar = swapped(0, "row", 2, xgive)
    x1, g1 = work(0, to_core, x0, xfar), work(0, to_core, g0, gfar)
    mask_in = work(0, lambda: kept_tiles(
        pattern_in, row_index * feat_tiles, feat_tiles, col_index * unit_tiles, unit_tiles
    ))
    mask_out = work(0, lambda: kept_tiles(
        pattern_out, col_index * unit_tiles, unit_tiles, row_index * feat_tiles, feat_tiles
    ))
    in_e = work(0, lambda mask: keep(w_in, mask), mask_in)
    x2 = work(0, lambda v, w: to_core(*lax.optimization_barrier((v, v[1], w))[:2]), xline0, in_e)
    core = swapped(0, "row", 1, work(0, lambda *v: jnp.stack([w[1] for w in v]), x1, x2, g1))
    xown, xline0, gown = [
        work(0, lambda v, got, n=n: jnp.stack([v[0], got[n]])[None], v, core)
        for n, v in enumerate((x1, x2, g1))
    ]

    out_e = work(2, lambda mask: keep(w_out, mask), mask_out)

    def give_half(*parts):
        return jnp.concatenate([v[v.shape[0] // 2 :] for v in parts]).astype(BF16)

    def add_half(*parts):
        kept = jnp.concatenate([v[: v.shape[0] // 2] for v in parts[:-1]])
        return kept + parts[-1].astype(F32)

    def row_sum(stages, parts, sizes):
        begin, core_stage, back, unpack = stages
        got = swapped(core_stage, "row", 1, work(begin, give_half, *parts))
        pair = work(core_stage, add_half, *parts, got)
        rounded = work(core_stage, to_bf16, pair)
        far = swapped(core_stage, "row", 2, rounded)
        total = work(back, lambda v, got: (v + got.astype(F32)).astype(BF16), pair, far)
        other = swapped(back, "row", 1, total)
        sums, start = [], 0
        for size in sizes:
            rows = slice(start, start + size)
            start = rows.stop
            sums.append(work(
                unpack,
                lambda v, got, rows=rows: jnp.concatenate([v[rows], got[rows]]).astype(F32),
                total,
                other,
            ))
        return sums, rounded

    def chunk(*parts):
        return jnp.concatenate(parts).swapaxes(0, 1).reshape(-1, feat)

    def join(*parts):
        return jnp.concatenate(parts)

    def behind(value, *others):
        return lax.optimization_barrier((value,) + others)[0]

    near = swapped(2, "col", 1, work(2, join, xown, xline0))
    xline, gline = [xline0], []
    xfirst, xnear = work(2, lambda v: v[:1], near), [work(2, lambda v: v[1:], near)]
    gfirst, gnear = swapped(2, "col", 1, gown), []
    xheld, gheld = [xown, xline0], [gown]
    for i in range(1, last):
        xline.append(swapped(1 + i, "col", line[i], work(1 + i, join, *xheld)))
        xheld.append(xline[i])
    gline.append(swapped(2, "col", line[0], gown))
    gheld.append(gline[0])
    sizes = [n * 4 * tok for n in places]
    xc = [work(2, chunk, xown, xfirst, xline[0], xnear[0])]
    xp = [work(2, product, xc[0], in_e)]
    (total,), rounded = row_sum((2, 3, 4, 4), xp, sizes[:1])
    pre = [total]
    for i in range(1, last):
        gnear.append(swapped(2 + i, "col", 1, gline[i - 1]))
        xnear.append(swapped(2 + i, "col", 1, xline[i]))
        held = work(2 + i, join, *gheld)
        gline.append(swapped(2 + i, "col", line[i], work(2 + i, behind, held, rounded)))
        gheld.append(gline[i])
    out_t = work(3, turn, out_e)
    gc = [work(3, chunk, gown, gfirst, gline[0], gnear[0])]
    gp = [work(3, product, gc[0], out_t)]
    gnear.append(swapped(4, "col", 1, gline[-1]))
    d_act = []
    for i in range(1, last):
        xc.append(work(4, chunk, xline[i], xnear[i]))
        xp.append(work(4, product, xc[i], in_e))
        sums, rounded = row_sum(
            (4, 4, 5, 5), [xp[i], gp[i - 1]], [sizes[i], sizes[i - 1]]
        )
        pre.append(sums[0])
        d_act.append(sums[1])
        late = work(4, behind, gline[i], rounded)
        gc.append(work(4, chunk, late, gnear[i]))
        gp.append(work(4, product, gc[i], out_t))
    in_t = work(4, turn, in_e)
    d_act.append(row_sum((4, 5, 6, 6), gp[-1:], sizes[-1:])[0][0])

    def forward(pre):
        value, slope = gelu_and_slope(pre)
        return value.astype(BF16), slope

    def places_first(value):
        return value.reshape(2, -1, 2 * tok, value.shape[-1]).swapaxes(0, 1)

    def give_near(i, v):
        v = places_first(v)
        return (v[v.shape[0] // 2 :] if i else v[1::2]).astype(BF16)

    def keep_near(i, v, got):
        v = places_first(v)
        return (v[: v.shape[0] // 2] if i else v[::2]) + got.astype(F32)

    made = [work(4 + i, forward, pre[i]) for i in range(last)]
    act = [work(4 + i, first, made[i]) for i in range(last)]
    yp = [work(4 + i, product, act[i], out_e) for i in range(last)]
    ygive = [work(4 + i, functools.partial(give_near, i), yp[i]) for i in range(last)]
    ynear = [swapped(4 + i, "col", 1, ygive[i]) for i in range(last)]
    d_pre = [
        work(5 + i, lambda v, made: (v * made[1]).astype(BF16), d_act[i], made[i])
        for i in range(last)
    ]
    np_ = [work(5 + i, product, d_pre[i], in_t) for i in range(last)]
    last_give = work(4 + last, functools.partial(give_near, last - 1), np_[-1])

    def add(v, got):
        return v + got

    def gain_terms(*parts):
        left, right = parts[:last], parts[last:]
        return sum(jnp.sum(n * x.astype(F32), axis=0) for n, x in zip(left, right))

    gain = work(6, gain_terms, *np_, *xc)
    for b, distance in enumerate([1] + line[::-1]):
        gain = work(7 if b < last else 8, add, gain, swapped(min(6 + b, 7), "col", distance, gain))
    got = swapped(8, "row", 1, gain)
    gain = work(8, lambda v, got: ordered(v, got, core_bit, 0), gain, got)
    got = swapped(8, "row", 2, gain)
    gain_gradient = work(
        8, lambda v, got: ordered(v, got, far_bit, 0) / layer_norm_gain, gain, got
    )

    nnear = [
        swapped(7, "col", 1, work(7, functools.partial(give_near, i), np_[i]))
        for i in range(last - 1)
    ] + [swapped(4 + last, "col", 1, last_give)]

    def line_sum(stage, products, got, late):
        sums, gives = [
            work(
                stage if i or not late else stage + last - 1,
                functools.partial(keep_near, i),
                products[i],
                got[i],
            )
            for i in range(last)
        ], []
        for i in reversed(range(1, last)):
            when = stage + last - 1 - i
            gives.append(work(when, to_bf16, sums[i]))
            moved = swapped(when, "col", line[i], gives[-1])
            for m in range(i):
                start = sum(places[:m])
                sums[m] = work(
                    when + 1,
                    lambda v, got, start=start: v + got[start : start + v.shape[0]].astype(F32),
                    sums[m],
                    moved,
                )
        return sums[0], gives[0]

    y, _ = line_sum(6, yp, ynear, False)
    moved = swapped(7, "col", line[0], work(7, lambda v: v[1].astype(BF16), y))
    y = work(8, lambda v, got: (v[0] + got.astype(F32)).astype(BF16), y, moved)
    got = swapped(8, "row", 1, work(8, second, y))
    y = work(8, lambda v, got: halves(ordered(v[0], got, core_bit, 1), far_bit, 0), y, got)
    got = swapped(8, "row", 2, work(8, second, y))
    output = work(9, lambda v, got: (
        inputs.astype(F32) + ordered(v[0], got, far_bit, 1).astype(F32)
    ).astype(BF16), y, got)

    n, last_sent = line_sum(7, np_, nnear, True)
    got = swapped(8, "row", 1, work(8, lambda v: v[:, 1].astype(BF16), n))
    n = work(
        8,
        lambda v, got: halves(ordered(v[:, 0], got.astype(F32), core_bit, 2), far_bit, 1),
        n,
        got,
    )
    own_line = swapped(8, "col", line[0], work(8, lambda v: v[0][1].astype(BF16), n))
    far_line = across(8, work(8, lambda v: v[1][1].astype(BF16), n))
    far_own = swapped(8, "row", 2, work(8, lambda v: v[1][0].astype(BF16), n))

    def input_gradient(v, own_line, far_own, far_line, made):
        standard, deviation = made[2:]
        mine = v[0][0] + own_line.astype(F32)
        other = far_own.astype(F32) + far_line.astype(F32)
        scaled = ordered(mine, other, far_bit, 1) * layer_norm_gain[None, :]
        result = deviation * (
            scaled
            - jnp.mean(scaled, axis=1, keepdims=True)
            - standard * jnp.mean(scaled * standard, axis=1, keepdims=True)
        )
        return (out_grad.astype(F32) + result).astype(BF16)

    grad_inputs = work(9, input_gradient, n, own_line, far_own, far_line, x0)

    def weight_gradient(mask, before, *parts):
        left, right = parts[:last], parts[last:]
        return outer(jnp.concatenate(left), jnp.concatenate(right), behind(mask, before))

    grad_w_out = work(4 + last, weight_gradient, mask_out, last_give, *act, *gc)
    grad_w_in = work(7, weight_gradient, mask_in, last_sent, *xc, *d_pre)

    return plan.run((output, grad_inputs, grad_w_in, grad_w_out, gain_gradient))


def solution(mesh):
    in_specs = (
        P(("row", "col"), None),
        P(),
        P("row", "col"),
        P("col", "row"),
        P(),
        P(),
        P(("row", "col"), None),
    )
    out_specs = (
        P(("row", "col"), None),
        P(("row", "col"), None),
        P("row", "col"),
        P("col", "row"),
        P(),
    )
    return jax.shard_map(shards, mesh=mesh, in_specs=in_specs, out_specs=out_specs, check_vma=False)
```

```python
import functools

import jax
import jax.numpy as jnp
from jax import lax
from jax.experimental import pallas as pl
from jax.experimental.pallas import tpu as pltpu
from jax.sharding import PartitionSpec as P

BLOCK = 256
PANEL = 1024
BF16 = jnp.bfloat16
F32 = jnp.float32
VMEM = pl.BlockSpec(memory_space=pltpu.VMEM)
SMEM = pl.BlockSpec(memory_space=pltpu.SMEM)
NO_COST = pl.CostEstimate(flops=0, bytes_accessed=0, transcendentals=0)


def kept_tiles(pattern, first_row, rows, first_column, columns):
    own = lax.dynamic_slice_in_dim(pattern, first_column, columns, 0)
    iota = first_row + jnp.arange(rows, dtype=jnp.int32)
    return jnp.any(own[None, :, :] == iota[:, None, None], axis=2).astype(jnp.int32)


def masked(keep_tile, value):
    return jnp.where(keep_tile == 1, value, jnp.zeros_like(value))


def keep_kernel(mask_ref, weight_ref, out_ref, copied):
    rows, columns = mask_ref.shape

    def each(kept, other):
        @pl.loop(0, rows)
        def _(i):
            for j in range(columns):
                here = (pl.ds(pl.multiple_of(i * BLOCK, BLOCK), BLOCK), pl.ds(j * BLOCK, BLOCK))

                @pl.when(mask_ref[i, j] == 1)
                def _():
                    kept(pltpu.make_async_copy(weight_ref.at[here], out_ref.at[here], copied.at[i, j]))

                if other is not None:

                    @pl.when(mask_ref[i, j] != 1)
                    def _():
                        other(here)

    def clear(here):
        out_ref[here] = jnp.zeros((BLOCK, BLOCK), out_ref.dtype)

    each(lambda copy: copy.start(), clear)
    each(lambda copy: copy.wait(), None)


def keep(weight, mask):
    return pl.pallas_call(
        keep_kernel,
        out_shape=pltpu.VMEM(weight.shape, weight.dtype),
        in_specs=[SMEM, pl.BlockSpec(memory_space=pltpu.HBM)],
        out_specs=VMEM,
        scratch_shapes=[pltpu.SemaphoreType.DMA(mask.shape)],
        compiler_params=pltpu.CompilerParams(vmem_limit_bytes=2 << 20),
        cost_estimate=NO_COST,
    )(mask, pltpu.with_memory_space_constraint(weight, pltpu.HBM))


def product_kernel(left_ref, weight_ref, out_ref):
    width = weight_ref.shape[1]
    panel = min(PANEL, width)

    @pl.loop(0, width // panel)
    def _(k):
        here = pl.ds(pl.multiple_of(k * panel, panel), panel)
        out_ref[:, here] = jnp.dot(
            left_ref[...], weight_ref[:, here], preferred_element_type=F32
        )


def product(left, weight):
    return pl.pallas_call(
        product_kernel,
        out_shape=jax.ShapeDtypeStruct((left.shape[0], weight.shape[1]), F32),
        in_specs=[VMEM, VMEM],
        out_specs=VMEM,
        compiler_params=pltpu.CompilerParams(vmem_limit_bytes=6 << 20),
        cost_estimate=NO_COST,
    )(left, pltpu.with_memory_space_constraint(weight, pltpu.VMEM))


def outer_kernel(mask_ref, left_ref, right_ref, out_ref):
    i = pl.program_id(0)
    tiles = out_ref.shape[0] // BLOCK
    turned = left_ref[...].T
    for j in range(out_ref.shape[1] // BLOCK):
        here = slice(j * BLOCK, (j + 1) * BLOCK)
        full = jnp.dot(turned, right_ref[:, here], preferred_element_type=F32)
        for t in range(tiles):
            rows = slice(t * BLOCK, (t + 1) * BLOCK)
            out_ref[rows, here] = masked(mask_ref[i * tiles + t, j], full[rows]).astype(
                out_ref.dtype
            )


def outer(left, right, mask):
    tokens, rows = left.shape
    columns = right.shape[1]
    step = 2 * BLOCK
    return pl.pallas_call(
        outer_kernel,
        grid=(rows // step,),
        out_shape=jax.ShapeDtypeStruct((rows, columns), BF16),
        in_specs=[
            SMEM,
            pl.BlockSpec((tokens, step), lambda i: (0, i)),
            pl.BlockSpec((tokens, columns), lambda i: (0, 0)),
        ],
        out_specs=pl.BlockSpec((step, columns), lambda i: (i, 0)),
        compiler_params=pltpu.CompilerParams(vmem_limit_bytes=12 << 20),
        cost_estimate=NO_COST,
    )(mask, left, right)


def normalise_kernel(
    far_ref, input_hbm, gain_hbm, kept_ref, given_ref, standard_ref, deviation_ref, input_ref, gain_ref, copied
):
    copies = [
        pltpu.make_async_copy(input_hbm, input_ref, copied.at[0]),
        pltpu.make_async_copy(gain_hbm, gain_ref, copied.at[1]),
    ]
    for copy in copies:
        copy.start()
    for copy in copies:
        copy.wait()
    xfloat = input_ref[...].astype(F32)
    centered = xfloat - jnp.mean(xfloat, axis=1, keepdims=True)
    deviation = lax.rsqrt(jnp.mean(centered * centered, axis=1, keepdims=True) + 1e-05)
    standard = centered * deviation
    normed = standard * gain_ref[...]
    half = normed.shape[1] // 2
    low, high = normed[:, :half], normed[:, half:]
    far = far_ref[0] == 1
    kept_ref[...] = jnp.where(far, high, low).astype(BF16)
    given_ref[...] = jnp.where(far, low, high).astype(BF16)
    standard_ref[...] = standard
    deviation_ref[...] = deviation


def normalise(inputs, gain, far):
    tok, width = inputs.shape
    half = jax.ShapeDtypeStruct((tok, width // 2), BF16)
    return pl.pallas_call(
        normalise_kernel,
        out_shape=(
            half,
            half,
            jax.ShapeDtypeStruct((tok, width), F32),
            jax.ShapeDtypeStruct((tok, 1), F32),
        ),
        in_specs=[SMEM] + [pl.BlockSpec(memory_space=pltpu.HBM)] * 2,
        out_specs=(VMEM,) * 4,
        scratch_shapes=[
            pltpu.VMEM(inputs.shape, inputs.dtype),
            pltpu.VMEM(gain.shape, gain.dtype),
            pltpu.SemaphoreType.DMA((2,)),
        ],
        compiler_params=pltpu.CompilerParams(vmem_limit_bytes=6 << 20),
        cost_estimate=NO_COST,
    )(far, *(pltpu.with_memory_space_constraint(v, pltpu.HBM) for v in (inputs, gain)))


def turn_kernel(weight_ref, out_ref):
    columns = weight_ref.shape[1]

    @pl.loop(0, columns // BLOCK)
    def _(k):
        here = pl.ds(pl.multiple_of(k * BLOCK, BLOCK), BLOCK)
        out_ref[here, :] = weight_ref[:, here].T


def turn(weight):
    return pl.pallas_call(
        turn_kernel,
        out_shape=pltpu.VMEM(weight.shape[::-1], weight.dtype),
        in_specs=[VMEM],
        out_specs=VMEM,
        compiler_params=pltpu.CompilerParams(vmem_limit_bytes=6 << 20),
        cost_estimate=NO_COST,
    )(pltpu.with_memory_space_constraint(weight, pltpu.VMEM))


def gelu_and_slope(h):
    tanh_v = jnp.tanh(0.7978845608 * (h + 0.044715 * h * h * h))
    value = 0.5 * h * (1.0 + tanh_v)
    slope = 0.5 * (1.0 + tanh_v) + 0.5 * h * (1.0 - tanh_v * tanh_v) * 0.7978845608 * (
        1.0 + 0.134145 * h * h
    )
    return value, slope


def swap(value, axis, distance):
    size = lax.axis_size(axis)
    return lax.ppermute(value, axis, [(i, i ^ distance) for i in range(size)])


def halves(value, bit, axis):
    low, high = jnp.split(value, 2, axis=axis)
    return jnp.where(bit, high, low), jnp.where(bit, low, high)


def ordered(mine, other, bit, axis):
    return jnp.where(
        bit,
        jnp.concatenate([other, mine], axis=axis),
        jnp.concatenate([mine, other], axis=axis),
    )


class Plan:
    def __init__(self, staged):
        self.staged = staged
        self.tasks = []
        self.first = set()

    def work(self, stage, function, *deps):
        self.tasks.append((stage if self.staged else 0, function, deps))
        return len(self.tasks) - 1

    def swap(self, stage, axis, distance, dep, urgent=False):
        if urgent:
            self.first.add(len(self.tasks))
        return self.work(stage, functools.partial(swap, axis=axis, distance=distance), dep)

    def run(self, results):
        values = {}
        for stage in sorted({t[0] for t in self.tasks}):
            for task, (when, function, deps) in enumerate(self.tasks):
                if when == stage:
                    values[task] = function(*(values[d] for d in deps))
            wanted = {d for when, _, deps in self.tasks if when > stage for d in deps}
            live = (wanted | set(results)) & set(values)
            live = sorted(live, key=lambda t: (t not in self.first, t))
            values.update(zip(live, lax.optimization_barrier(tuple(values[n] for n in live))))
        return tuple(values[n] for n in results)


def first(pair):
    return pair[0]


def second(pair):
    return pair[1]


def to_bf16(value):
    return value.astype(BF16)


def shards(inputs, layer_norm_gain, w_in, w_out, pattern_in, pattern_out, out_grad):
    n_col = lax.axis_size("col")
    row_index = lax.axis_index("row")
    col_index = lax.axis_index("col")
    core_bit = row_index % 2 == 1
    far_bit = row_index // 2 == 1
    tok = inputs.shape[0]
    feat, unit = w_in.shape
    feat_tiles, unit_tiles = feat // BLOCK, unit // BLOCK
    line = [1 << b for b in reversed(range(1, n_col.bit_length() - 1))]
    last = len(line)
    places = [2] + [1 << i for i in range(1, last)]

    plan = Plan(last == 2)
    work, swapped = plan.work, plan.swap

    def to_core(v, got):
        return halves(ordered(v[0], got, far_bit, 0), core_bit, 1)

    def across(stage, dep):
        return swapped(stage, ("row", "col"), 2 * n_col + line[0], dep)

    g0 = work(0, lambda: halves(out_grad, far_bit, 1))
    gfar = swapped(0, "row", 2, work(0, second, g0))
    x0 = work(
        0,
        lambda: normalise(inputs, layer_norm_gain[None, :], far_bit.astype(jnp.int32)[None]),
    )
    xgive = work(0, second, x0)
    xline0 = work(
        0,
        lambda v, got: (v,  got),
        swapped(0, "col", line[0], work(0, first, x0)),
        across(0, xgive),
    )
    xfar = swapped(0, "row", 2, xgive)
    x1, g1 = work(0, to_core, x0, xfar), work(0, to_core, g0, gfar)
    mask_in = work(0, lambda: kept_tiles(
        pattern_in, row_index * feat_tiles, feat_tiles, col_index * unit_tiles, unit_tiles
    ))
    mask_out = work(0, lambda: kept_tiles(
        pattern_out, col_index * unit_tiles, unit_tiles, row_index * feat_tiles, feat_tiles
    ))
    in_e = work(0, lambda mask: keep(w_in, mask), mask_in)
    x2 = work(0, lambda v, w: to_core(*lax.optimization_barrier((v, v[1], w))[:2]), xline0, in_e)
    core = swapped(0, "row", 1, work(0, lambda *v: jnp.stack([w[1] for w in v]), x1, x2, g1))
    xown, xline0, gown = [
        work(0, lambda v, got, n=n: jnp.stack([v[0], got[n]])[None], v, core)
        for n, v in enumerate((x1, x2, g1))
    ]

    out_e = work(2, lambda mask: keep(w_out, mask), mask_out)

    def give_half(*parts):
        return jnp.concatenate([v[v.shape[0] // 2 :] for v in parts]).astype(BF16)

    def add_half(*parts):
        kept = jnp.concatenate([v[: v.shape[0] // 2] for v in parts[:-1]])
        return kept + parts[-1].astype(F32)

    def row_sum(stages, parts, sizes):
        begin, core_stage, back, unpack = stages
        got = swapped(core_stage, "row", 1, work(begin, give_half, *parts))
        pair = work(core_stage, add_half, *parts, got)
        rounded = work(core_stage, to_bf16, pair)
        far = swapped(core_stage, "row", 2, rounded)
        total = work(back, lambda v, got: (v + got.astype(F32)).astype(BF16), pair, far)
        other = swapped(back, "row", 1, total)
        sums, start = [], 0
        for size in sizes:
            rows = slice(start, start + size)
            start = rows.stop
            sums.append(work(
                unpack,
                lambda v, got, rows=rows: jnp.concatenate([v[rows], got[rows]]).astype(F32),
                total,
                other,
            ))
        return sums, rounded

    def chunk(*parts):
        return jnp.concatenate(parts).swapaxes(0, 1).reshape(-1, feat)

    def join(*parts):
        return jnp.concatenate(parts)

    def behind(value, *others):
        return lax.optimization_barrier((value,) + others)[0]

    near = swapped(2, "col", 1, work(2, join, xown, xline0))
    xline, gline = [xline0], []
    xfirst, xnear = work(2, lambda v: v[:1], near), [work(2, lambda v: v[1:], near)]
    gfirst, gnear = swapped(2, "col", 1, gown), []
    xheld, gheld = [xown, xline0], [gown]
    for i in range(1, last):
        xline.append(swapped(1 + i, "col", line[i], work(1 + i, join, *xheld)))
        xheld.append(xline[i])
    gline.append(swapped(2, "col", line[0], gown))
    gheld.append(gline[0])
    sizes = [n * 4 * tok for n in places]
    xc = [work(2, chunk, xown, xfirst, xline[0], xnear[0])]
    xp = [work(2, product, xc[0], in_e)]
    (total,), rounded = row_sum((2, 3, 4, 4), xp, sizes[:1])
    pre = [total]
    for i in range(1, last):
        gnear.append(swapped(2 + i, "col", 1, gline[i - 1]))
        xnear.append(swapped(2 + i, "col", 1, xline[i]))
        held = work(2 + i, join, *gheld)
        gline.append(swapped(2 + i, "col", line[i], work(2 + i, behind, held, rounded)))
        gheld.append(gline[i])
    out_t = work(3, turn, out_e)
    gc = [work(3, chunk, gown, gfirst, gline[0], gnear[0])]
    gp = [work(3, product, gc[0], out_t)]
    plan.first |= {gc[0], gp[0]}
    gnear.append(swapped(4, "col", 1, gline[-1]))
    d_act = []
    for i in range(1, last):
        xc.append(work(4, chunk, xline[i], xnear[i]))
        xp.append(work(4, product, xc[i], in_e))
        sums, rounded = row_sum(
            (4, 4, 5, 5), [xp[i], gp[i - 1]], [sizes[i], sizes[i - 1]]
        )
        pre.append(sums[0])
        d_act.append(sums[1])
        late = work(4, behind, gline[i], rounded)
        gc.append(work(4, chunk, late, gnear[i]))
        gp.append(work(4, product, gc[i], out_t))
    in_t = work(4, turn, in_e)
    d_act.append(row_sum((4, 5, 6, 6), gp[-1:], sizes[-1:])[0][0])

    def forward(pre):
        value, slope = gelu_and_slope(pre)
        return value.astype(BF16), slope

    def places_first(value):
        return value.reshape(2, -1, 2 * tok, value.shape[-1]).swapaxes(0, 1)

    def give_near(i, v):
        v = places_first(v)
        return (v[v.shape[0] // 2 :] if i else v[1::2]).astype(BF16)

    def keep_near(i, v, got):
        v = places_first(v)
        return (v[: v.shape[0] // 2] if i else v[::2]) + got.astype(F32)

    made = [work(4 + i, forward, pre[i]) for i in range(last)]
    act = [work(4 + i, first, made[i]) for i in range(last)]
    yp = [work(4 + i, product, act[i], out_e) for i in range(last)]
    ygive = [work(4 + i, functools.partial(give_near, i), yp[i]) for i in range(last)]
    ynear = [swapped(4 + i, "col", 1, ygive[i]) for i in range(last)]
    d_pre = [
        work(5 + i, lambda v, made: (v * made[1]).astype(BF16), d_act[i], made[i])
        for i in range(last)
    ]
    np_ = [work(5 + i, product, d_pre[i], in_t) for i in range(last)]
    last_give = work(4 + last, functools.partial(give_near, last - 1), np_[-1])

    def add(v, got):
        return v + got

    def gain_terms(*parts):
        left, right = parts[:last], parts[last:]
        return sum(jnp.sum(n * x.astype(F32), axis=0) for n, x in zip(left, right))

    gain = work(6, gain_terms, *np_, *xc)
    for distance in [1] + line[:0:-1]:
        gain = work(6, add, gain, swapped(6, "col", distance, gain))
    gain = work(8, add, gain, swapped(7, "col", line[0], gain))
    got = swapped(8, "row", 1, gain)
    gain = work(8, lambda v, got: ordered(v, got, core_bit, 0), gain, got)
    got = swapped(8, "row", 2, gain)
    gain_gradient = work(
        8, lambda v, got: ordered(v, got, far_bit, 0) / layer_norm_gain, gain, got
    )

    nnear = [
        swapped(7, "col", 1, work(7, functools.partial(give_near, i), np_[i]))
        for i in range(last - 1)
    ] + [swapped(4 + last, "col", 1, last_give, True)]

    def line_sum(stage, products, got, late):
        sums, gives = [
            work(
                stage if i or not late else stage + last - 1,
                functools.partial(keep_near, i),
                products[i],
                got[i],
            )
            for i in range(last)
        ], []
        for i in reversed(range(1, last)):
            when = stage + last - 1 - i
            gives.append(work(when, to_bf16, sums[i]))
            moved = swapped(when, "col", line[i], gives[-1], late)
            for m in range(i):
                start = sum(places[:m])
                sums[m] = work(
                    when + 1,
                    lambda v, got, start=start: v + got[start : start + v.shape[0]].astype(F32),
                    sums[m],
                    moved,
                )
        return sums[0], gives[0]

    y, _ = line_sum(6, yp, ynear, False)
    moved = swapped(7, "col", line[0], work(7, lambda v: v[1].astype(BF16), y))
    y = work(8, lambda v, got: (v[0] + got.astype(F32)).astype(BF16), y, moved)
    got = swapped(8, "row", 1, work(8, second, y))
    y = work(8, lambda v, got: halves(ordered(v[0], got, core_bit, 1), far_bit, 0), y, got)
    got = swapped(8, "row", 2, work(8, second, y))
    output = work(9, lambda v, got: (
        inputs.astype(F32) + ordered(v[0], got, far_bit, 1).astype(F32)
    ).astype(BF16), y, got)

    n, last_sent = line_sum(7, np_, nnear, True)
    got = swapped(8, "row", 1, work(8, lambda v: v[:, 1].astype(BF16), n))
    n = work(
        8,
        lambda v, got: halves(ordered(v[:, 0], got.astype(F32), core_bit, 2), far_bit, 1),
        n,
        got,
    )
    own_line = swapped(8, "col", line[0], work(8, lambda v: v[0][1].astype(BF16), n))
    far_line = across(8, work(8, lambda v: v[1][1].astype(BF16), n))
    far_own = swapped(8, "row", 2, work(8, lambda v: v[1][0].astype(BF16), n))

    def input_gradient(v, own_line, far_own, far_line, made):
        standard, deviation = made[2:]
        mine = v[0][0] + own_line.astype(F32)
        other = far_own.astype(F32) + far_line.astype(F32)
        scaled = ordered(mine, other, far_bit, 1) * layer_norm_gain[None, :]
        result = deviation * (
            scaled
            - jnp.mean(scaled, axis=1, keepdims=True)
            - standard * jnp.mean(scaled * standard, axis=1, keepdims=True)
        )
        return (out_grad.astype(F32) + result).astype(BF16)

    grad_inputs = work(9, input_gradient, n, own_line, far_own, far_line, x0)

    def weight_gradient(mask, before, *parts):
        left, right = parts[:last], parts[last:]
        return outer(jnp.concatenate(left), jnp.concatenate(right), behind(mask, before))

    grad_w_out = work(5, weight_gradient, mask_out, ygive[-1], *act, *gc)
    grad_w_in = work(7, weight_gradient, mask_in, last_sent, *xc, *d_pre)

    return plan.run((output, grad_inputs, grad_w_in, grad_w_out, gain_gradient))


def solution(mesh):
    in_specs = (
        P(("row", "col"), None),
        P(),
        P("row", "col"),
        P("col", "row"),
        P(),
        P(),
        P(("row", "col"), None),
    )
    out_specs = (
        P(("row", "col"), None),
        P(("row", "col"), None),
        P("row", "col"),
        P("col", "row"),
        P(),
    )
    return jax.shard_map(shards, mesh=mesh, in_specs=in_specs, out_specs=out_specs, check_vma=False)
```

```python
import functools

import jax
import jax.numpy as jnp
from jax import lax
from jax.experimental import pallas as pl
from jax.experimental.pallas import tpu as pltpu
from jax.sharding import PartitionSpec as P

BLOCK = 256
PANEL = 1024
BF16 = jnp.bfloat16
F32 = jnp.float32
VMEM = pl.BlockSpec(memory_space=pltpu.VMEM)
SMEM = pl.BlockSpec(memory_space=pltpu.SMEM)
NO_COST = pl.CostEstimate(flops=0, bytes_accessed=0, transcendentals=0)


def kept_tiles(pattern, first_row, rows, first_column, columns):
    own = lax.dynamic_slice_in_dim(pattern, first_column, columns, 0)
    iota = first_row + jnp.arange(rows, dtype=jnp.int32)
    return jnp.any(own[None, :, :] == iota[:, None, None], axis=2).astype(jnp.int32)


def masked(keep_tile, value):
    return jnp.where(keep_tile == 1, value, jnp.zeros_like(value))


def keep_kernel(mask_ref, weight_ref, out_ref, copied):
    rows, columns = mask_ref.shape

    def each(kept, other):
        @pl.loop(0, rows)
        def _(i):
            for j in range(columns):
                here = (pl.ds(pl.multiple_of(i * BLOCK, BLOCK), BLOCK), pl.ds(j * BLOCK, BLOCK))

                @pl.when(mask_ref[i, j] == 1)
                def _():
                    kept(pltpu.make_async_copy(weight_ref.at[here], out_ref.at[here], copied.at[i, j]))

                if other is not None:

                    @pl.when(mask_ref[i, j] != 1)
                    def _():
                        other(here)

    def clear(here):
        out_ref[here] = jnp.zeros((BLOCK, BLOCK), out_ref.dtype)

    each(lambda copy: copy.start(), clear)
    each(lambda copy: copy.wait(), None)


def keep(weight, mask):
    return pl.pallas_call(
        keep_kernel,
        out_shape=pltpu.VMEM(weight.shape, weight.dtype),
        in_specs=[SMEM, pl.BlockSpec(memory_space=pltpu.HBM)],
        out_specs=VMEM,
        scratch_shapes=[pltpu.SemaphoreType.DMA(mask.shape)],
        compiler_params=pltpu.CompilerParams(vmem_limit_bytes=2 << 20),
        cost_estimate=NO_COST,
    )(mask, pltpu.with_memory_space_constraint(weight, pltpu.HBM))


def product_kernel(left_ref, weight_ref, out_ref):
    width = weight_ref.shape[1]
    panel = min(PANEL, width)

    @pl.loop(0, width // panel)
    def _(k):
        here = pl.ds(pl.multiple_of(k * panel, panel), panel)
        out_ref[:, here] = jnp.dot(
            left_ref[...], weight_ref[:, here], preferred_element_type=F32
        )


def product(left, weight):
    return pl.pallas_call(
        product_kernel,
        out_shape=jax.ShapeDtypeStruct((left.shape[0], weight.shape[1]), F32),
        in_specs=[VMEM, VMEM],
        out_specs=VMEM,
        compiler_params=pltpu.CompilerParams(vmem_limit_bytes=6 << 20),
        cost_estimate=NO_COST,
    )(left, pltpu.with_memory_space_constraint(weight, pltpu.VMEM))


def outer_kernel(mask_ref, left_ref, right_ref, out_ref):
    i = pl.program_id(0)
    tiles = out_ref.shape[0] // BLOCK
    turned = left_ref[...].T
    for j in range(out_ref.shape[1] // BLOCK):
        here = slice(j * BLOCK, (j + 1) * BLOCK)
        full = jnp.dot(turned, right_ref[:, here], preferred_element_type=F32)
        for t in range(tiles):
            rows = slice(t * BLOCK, (t + 1) * BLOCK)
            out_ref[rows, here] = masked(mask_ref[i * tiles + t, j], full[rows]).astype(
                out_ref.dtype
            )


def outer(left, right, mask):
    tokens, rows = left.shape
    columns = right.shape[1]
    step = 2 * BLOCK
    return pl.pallas_call(
        outer_kernel,
        grid=(rows // step,),
        out_shape=jax.ShapeDtypeStruct((rows, columns), BF16),
        in_specs=[
            SMEM,
            pl.BlockSpec((tokens, step), lambda i: (0, i)),
            pl.BlockSpec((tokens, columns), lambda i: (0, 0)),
        ],
        out_specs=pl.BlockSpec((step, columns), lambda i: (i, 0)),
        compiler_params=pltpu.CompilerParams(vmem_limit_bytes=12 << 20),
        cost_estimate=NO_COST,
    )(mask, left, right)


def normalise_kernel(
    far_ref, input_hbm, gain_hbm, kept_ref, given_ref, standard_ref, deviation_ref, input_ref, gain_ref, copied
):
    copies = [
        pltpu.make_async_copy(input_hbm, input_ref, copied.at[0]),
        pltpu.make_async_copy(gain_hbm, gain_ref, copied.at[1]),
    ]
    for copy in copies:
        copy.start()
    for copy in copies:
        copy.wait()
    xfloat = input_ref[...].astype(F32)
    centered = xfloat - jnp.mean(xfloat, axis=1, keepdims=True)
    deviation = lax.rsqrt(jnp.mean(centered * centered, axis=1, keepdims=True) + 1e-05)
    standard = centered * deviation
    normed = standard * gain_ref[...]
    half = normed.shape[1] // 2
    low, high = normed[:, :half], normed[:, half:]
    far = far_ref[0] == 1
    kept_ref[...] = jnp.where(far, high, low).astype(BF16)
    given_ref[...] = jnp.where(far, low, high).astype(BF16)
    standard_ref[...] = standard
    deviation_ref[...] = deviation


def normalise(inputs, gain, far):
    tok, width = inputs.shape
    half = jax.ShapeDtypeStruct((tok, width // 2), BF16)
    return pl.pallas_call(
        normalise_kernel,
        out_shape=(
            half,
            half,
            jax.ShapeDtypeStruct((tok, width), F32),
            jax.ShapeDtypeStruct((tok, 1), F32),
        ),
        in_specs=[SMEM] + [pl.BlockSpec(memory_space=pltpu.HBM)] * 2,
        out_specs=(VMEM,) * 4,
        scratch_shapes=[
            pltpu.VMEM(inputs.shape, inputs.dtype),
            pltpu.VMEM(gain.shape, gain.dtype),
            pltpu.SemaphoreType.DMA((2,)),
        ],
        compiler_params=pltpu.CompilerParams(vmem_limit_bytes=6 << 20),
        cost_estimate=NO_COST,
    )(far, *(pltpu.with_memory_space_constraint(v, pltpu.HBM) for v in (inputs, gain)))


def turn_kernel(weight_ref, out_ref):
    columns = weight_ref.shape[1]

    @pl.loop(0, columns // BLOCK)
    def _(k):
        here = pl.ds(pl.multiple_of(k * BLOCK, BLOCK), BLOCK)
        out_ref[here, :] = weight_ref[:, here].T


def turn(weight):
    return pl.pallas_call(
        turn_kernel,
        out_shape=pltpu.VMEM(weight.shape[::-1], weight.dtype),
        in_specs=[VMEM],
        out_specs=VMEM,
        compiler_params=pltpu.CompilerParams(vmem_limit_bytes=6 << 20),
        cost_estimate=NO_COST,
    )(pltpu.with_memory_space_constraint(weight, pltpu.VMEM))


def gelu_and_slope(h):
    tanh_v = jnp.tanh(0.7978845608 * (h + 0.044715 * h * h * h))
    value = 0.5 * h * (1.0 + tanh_v)
    slope = 0.5 * (1.0 + tanh_v) + 0.5 * h * (1.0 - tanh_v * tanh_v) * 0.7978845608 * (
        1.0 + 0.134145 * h * h
    )
    return value, slope


def swap(value, axis, distance):
    size = lax.axis_size(axis)
    return lax.ppermute(value, axis, [(i, i ^ distance) for i in range(size)])


def halves(value, bit, axis):
    low, high = jnp.split(value, 2, axis=axis)
    return jnp.where(bit, high, low), jnp.where(bit, low, high)


def ordered(mine, other, bit, axis):
    return jnp.where(
        bit,
        jnp.concatenate([other, mine], axis=axis),
        jnp.concatenate([mine, other], axis=axis),
    )


class Plan:
    def __init__(self, staged):
        self.staged = staged
        self.tasks = []
        self.first = set()

    def work(self, stage, function, *deps):
        self.tasks.append((stage if self.staged else 0, function, deps))
        return len(self.tasks) - 1

    def swap(self, stage, axis, distance, dep, urgent=False):
        if urgent:
            self.first.add(len(self.tasks))
        return self.work(stage, functools.partial(swap, axis=axis, distance=distance), dep)

    def run(self, results):
        values = {}
        for stage in sorted({t[0] for t in self.tasks}):
            for task, (when, function, deps) in enumerate(self.tasks):
                if when == stage:
                    values[task] = function(*(values[d] for d in deps))
            wanted = {d for when, _, deps in self.tasks if when > stage for d in deps}
            live = (wanted | set(results)) & set(values)
            live = sorted(live, key=lambda t: (t not in self.first, t))
            values.update(zip(live, lax.optimization_barrier(tuple(values[n] for n in live))))
        return tuple(values[n] for n in results)


def first(pair):
    return pair[0]


def second(pair):
    return pair[1]


def to_bf16(value):
    return value.astype(BF16)


def shards(inputs, layer_norm_gain, w_in, w_out, pattern_in, pattern_out, out_grad):
    n_col = lax.axis_size("col")
    row_index = lax.axis_index("row")
    col_index = lax.axis_index("col")
    core_bit = row_index % 2 == 1
    far_bit = row_index // 2 == 1
    tok = inputs.shape[0]
    feat, unit = w_in.shape
    feat_tiles, unit_tiles = feat // BLOCK, unit // BLOCK
    line = [1 << b for b in reversed(range(1, n_col.bit_length() - 1))]
    last = len(line)
    places = [2] + [1 << i for i in range(1, last)]

    plan = Plan(last == 2)
    work, swapped = plan.work, plan.swap

    def to_core(v, got):
        return halves(ordered(v[0], got, far_bit, 0), core_bit, 1)

    def across(stage, dep):
        return swapped(stage, ("row", "col"), 2 * n_col + line[0], dep)

    g0 = work(0, lambda: halves(out_grad, far_bit, 1))
    gfar = swapped(0, "row", 2, work(0, second, g0))
    x0 = work(
        0,
        lambda: normalise(inputs, layer_norm_gain[None, :], far_bit.astype(jnp.int32)[None]),
    )
    xgive = work(0, second, x0)
    xline0 = work(
        0,
        lambda v, got: (v,  got),
        swapped(0, "col", line[0], work(0, first, x0)),
        across(0, xgive),
    )
    xfar = swapped(0, "row", 2, xgive)
    x1, g1 = work(0, to_core, x0, xfar), work(0, to_core, g0, gfar)
    mask_in = work(0, lambda: kept_tiles(
        pattern_in, row_index * feat_tiles, feat_tiles, col_index * unit_tiles, unit_tiles
    ))
    mask_out = work(0, lambda: kept_tiles(
        pattern_out, col_index * unit_tiles, unit_tiles, row_index * feat_tiles, feat_tiles
    ))
    in_e = work(0, lambda mask: keep(w_in, mask), mask_in)
    x2 = work(0, lambda v, w: to_core(*lax.optimization_barrier((v, v[1], w))[:2]), xline0, in_e)
    core = swapped(0, "row", 1, work(0, lambda *v: jnp.stack([w[1] for w in v]), x1, x2, g1))
    xown, xline0, gown = [
        work(0, lambda v, got, n=n: jnp.stack([v[0], got[n]])[None], v, core)
        for n, v in enumerate((x1, x2, g1))
    ]

    out_e = work(2, lambda mask: keep(w_out, mask), mask_out)

    def give_half(*parts):
        return jnp.concatenate([v[v.shape[0] // 2 :] for v in parts]).astype(BF16)

    def add_half(*parts):
        kept = jnp.concatenate([v[: v.shape[0] // 2] for v in parts[:-1]])
        return kept + parts[-1].astype(F32)

    def row_sum(stages, parts, sizes):
        begin, core_stage, back, unpack = stages
        got = swapped(core_stage, "row", 1, work(begin, give_half, *parts))
        pair = work(core_stage, add_half, *parts, got)
        rounded = work(core_stage, to_bf16, pair)
        far = swapped(core_stage, "row", 2, rounded)
        total = work(back, lambda v, got: (v + got.astype(F32)).astype(BF16), pair, far)
        other = swapped(back, "row", 1, total)
        sums, start = [], 0
        for size in sizes:
            rows = slice(start, start + size)
            start = rows.stop
            sums.append(work(
                unpack,
                lambda v, got, rows=rows: jnp.concatenate([v[rows], got[rows]]).astype(F32),
                total,
                other,
            ))
        return sums, rounded

    def chunk(*parts):
        return jnp.concatenate(parts).swapaxes(0, 1).reshape(-1, feat)

    def join(*parts):
        return jnp.concatenate(parts)

    def behind(value, *others):
        return lax.optimization_barrier((value,) + others)[0]

    near = swapped(2, "col", 1, work(2, join, xown, xline0))
    xline, gline = [xline0], []
    xfirst, xnear = work(2, lambda v: v[:1], near), [work(2, lambda v: v[1:], near)]
    gfirst, gnear = swapped(2, "col", 1, gown), []
    xheld, gheld = [xown, xline0], [gown]
    for i in range(1, last):
        xline.append(swapped(1 + i, "col", line[i], work(1 + i, join, *xheld), True))
        xheld.append(xline[i])
    gline.append(swapped(2, "col", line[0], gown))
    gheld.append(gline[0])
    sizes = [n * 4 * tok for n in places]
    xc = [work(2, chunk, xown, xfirst, xline[0], xnear[0])]
    xp = [work(2, product, xc[0], in_e)]
    (total,), rounded = row_sum((2, 3, 4, 4), xp, sizes[:1])
    pre = [total]
    for i in range(1, last):
        gnear.append(swapped(2 + i, "col", 1, gline[i - 1]))
        xnear.append(swapped(2 + i, "col", 1, xline[i]))
        held = work(2 + i, join, *gheld)
        gline.append(swapped(2 + i, "col", line[i], work(2 + i, behind, held, rounded)))
        gheld.append(gline[i])
    out_t = work(3, turn, out_e)
    gc = [work(3, chunk, gown, gfirst, gline[0], gnear[0])]
    gp = [work(3, product, gc[0], out_t)]
    plan.first |= {gc[0], gp[0]}
    gnear.append(swapped(4, "col", 1, gline[-1]))
    d_act = []
    for i in range(1, last):
        xc.append(work(4, chunk, xline[i], xnear[i]))
        xp.append(work(4, product, xc[i], in_e))
        sums, rounded = row_sum(
            (4, 4, 5, 5), [xp[i], gp[i - 1]], [sizes[i], sizes[i - 1]]
        )
        pre.append(sums[0])
        d_act.append(sums[1])
        late = work(4, behind, gline[i], rounded)
        gc.append(work(4, chunk, late, gnear[i]))
        gp.append(work(4, product, gc[i], out_t))
    in_t = work(4, turn, in_e)
    d_act.append(row_sum((4, 5, 6, 6), gp[-1:], sizes[-1:])[0][0])

    def forward(pre):
        value, slope = gelu_and_slope(pre)
        return value.astype(BF16), slope

    def places_first(value):
        return value.reshape(2, -1, 2 * tok, value.shape[-1]).swapaxes(0, 1)

    def give_near(i, v):
        v = places_first(v)
        return (v[v.shape[0] // 2 :] if i else v[1::2]).astype(BF16)

    def keep_near(i, v, got):
        v = places_first(v)
        return (v[: v.shape[0] // 2] if i else v[::2]) + got.astype(F32)

    made = [work(4 + i, forward, pre[i]) for i in range(last)]
    act = [work(4 + i, first, made[i]) for i in range(last)]
    yp = [work(4 + i, product, act[i], out_e) for i in range(last)]
    ygive = [work(4 + i, functools.partial(give_near, i), yp[i]) for i in range(last)]
    ynear = [swapped(4 + i, "col", 1, ygive[i]) for i in range(last)]
    d_pre = [
        work(5 + i, lambda v, made: (v * made[1]).astype(BF16), d_act[i], made[i])
        for i in range(last)
    ]
    np_ = [work(5 + i, product, d_pre[i], in_t) for i in range(last)]
    last_give = work(4 + last, functools.partial(give_near, last - 1), np_[-1])

    def add(v, got):
        return v + got

    def gain_terms(*parts):
        left, right = parts[:last], parts[last:]
        return sum(jnp.sum(n * x.astype(F32), axis=0) for n, x in zip(left, right))

    gain = work(6, gain_terms, *np_, *xc)
    for distance in [1] + line[:0:-1]:
        gain = work(6, add, gain, swapped(6, "col", distance, gain))
    gain = work(8, add, gain, swapped(7, "col", line[0], gain))
    got = swapped(8, "row", 1, gain)
    gain = work(8, lambda v, got: ordered(v, got, core_bit, 0), gain, got)
    got = swapped(8, "row", 2, gain)
    gain_gradient = work(
        8, lambda v, got: ordered(v, got, far_bit, 0) / layer_norm_gain, gain, got
    )

    nnear = [
        swapped(7, "col", 1, work(7, functools.partial(give_near, i), np_[i]))
        for i in range(last - 1)
    ] + [swapped(4 + last, "col", 1, last_give, True)]

    def line_sum(stage, products, got, late):
        sums, gives = [
            work(
                stage if i or not late else stage + last - 1,
                functools.partial(keep_near, i),
                products[i],
                got[i],
            )
            for i in range(last)
        ], []
        for i in reversed(range(1, last)):
            when = stage + last - 1 - i
            gives.append(work(when, to_bf16, sums[i]))
            moved = swapped(when, "col", line[i], gives[-1], late)
            for m in range(i):
                start = sum(places[:m])
                sums[m] = work(
                    when + 1,
                    lambda v, got, start=start: v + got[start : start + v.shape[0]].astype(F32),
                    sums[m],
                    moved,
                )
        return sums[0], gives[0]

    y, _ = line_sum(6, yp, ynear, False)
    moved = swapped(7, "col", line[0], work(7, lambda v: v[1].astype(BF16), y))
    y = work(8, lambda v, got: (v[0] + got.astype(F32)).astype(BF16), y, moved)
    got = swapped(8, "row", 1, work(8, second, y))
    y = work(8, lambda v, got: halves(ordered(v[0], got, core_bit, 1), far_bit, 0), y, got)
    got = swapped(8, "row", 2, work(8, second, y))
    output = work(9, lambda v, got: (
        inputs.astype(F32) + ordered(v[0], got, far_bit, 1).astype(F32)
    ).astype(BF16), y, got)

    n, last_sent = line_sum(7, np_, nnear, True)
    got = swapped(8, "row", 1, work(8, lambda v: v[:, 1].astype(BF16), n))
    n = work(
        8,
        lambda v, got: halves(ordered(v[:, 0], got.astype(F32), core_bit, 2), far_bit, 1),
        n,
        got,
    )
    own_line = swapped(8, "col", line[0], work(8, lambda v: v[0][1].astype(BF16), n))
    far_line = across(8, work(8, lambda v: v[1][1].astype(BF16), n))
    far_own = swapped(8, "row", 2, work(8, lambda v: v[1][0].astype(BF16), n))

    def input_gradient(v, own_line, far_own, far_line, made):
        standard, deviation = made[2:]
        mine = v[0][0] + own_line.astype(F32)
        other = far_own.astype(F32) + far_line.astype(F32)
        scaled = ordered(mine, other, far_bit, 1) * layer_norm_gain[None, :]
        result = deviation * (
            scaled
            - jnp.mean(scaled, axis=1, keepdims=True)
            - standard * jnp.mean(scaled * standard, axis=1, keepdims=True)
        )
        return (out_grad.astype(F32) + result).astype(BF16)

    grad_inputs = work(9, input_gradient, n, own_line, far_own, far_line, x0)

    def weight_gradient(mask, before, *parts):
        left, right = parts[:last], parts[last:]
        return outer(jnp.concatenate(left), jnp.concatenate(right), behind(mask, before))

    grad_w_out = work(5, weight_gradient, mask_out, ygive[-1], *act, *gc)
    grad_w_in = work(7, weight_gradient, mask_in, last_sent, *xc, *d_pre)

    return plan.run((output, grad_inputs, grad_w_in, grad_w_out, gain_gradient))


def solution(mesh):
    in_specs = (
        P(("row", "col"), None),
        P(),
        P("row", "col"),
        P("col", "row"),
        P(),
        P(),
        P(("row", "col"), None),
    )
    out_specs = (
        P(("row", "col"), None),
        P(("row", "col"), None),
        P("row", "col"),
        P("col", "row"),
        P(),
    )
    return jax.shard_map(shards, mesh=mesh, in_specs=in_specs, out_specs=out_specs, check_vma=False)
```
